256 devices in a mesh: wide: 64 (over x_lo, z, y), narrow: 4 (over x_hi, core).
Axes of the slice: x: 4 (x_hi: 2, x_lo: 2; x = x_hi * 2 + x_lo), y: 4, z: 8, core: 2. Of those that a mesh axis runs over, the one named last changes fastest.
Arguments:
- field: bfloat16 [2, 512, 512, 512], P(None, 'wide', 'narrow'), may hold values from -20 to 20
- gain: float32 [512, 512], P('wide', 'narrow'), may hold values from 0.2 to 1
- spectral_phase: float32 [512], replicated, may hold values from -3.140625 to 3.140625
Outputs:
- field_out: bfloat16 [2, 512, 512, 512], P(None, 'wide', 'narrow')
The draws below stay inside these ranges and needn't reach their ends.
All inputs are finite; a program needn't handle non-finite values.
Results may differ from the reference program's by a relative error of at most 0.017.
Values may be sent and summed in bfloat16 or wider, within the bound.
A program may use at most 64 MiB of HBM per device.

```python
import math
import jax
import jax.numpy as jnp
from jax import lax

NX = 512
NY = 512
NT = 512


def draw_field(key, part):
    key = jax.random.fold_in(key, 7)
    base_key, pixel_key, time_key, tone_key, beam_key = jax.random.split(key, 5)
    base = jnp.clip(jax.random.normal(base_key, (2, NX, NY, NT), jnp.float32), -5.0, 5.0)
    tone = jnp.clip(jax.random.normal(tone_key, (2, NT), jnp.float32), -4.0, 4.0)
    lowest = 0.5
    highest = 2.0
    beam_level = 2.0
    pixel_scale = jnp.exp(jax.random.uniform(pixel_key, (NX, NY), jnp.float32, jnp.log(lowest), jnp.log(highest)))
    time_scale = jnp.exp(jax.random.uniform(time_key, (NT,), jnp.float32, jnp.log(lowest), jnp.log(highest)))
    phases = jax.random.uniform(beam_key, (2,), jnp.float32, -math.pi, math.pi)
    x_index = jnp.arange(NX, dtype=jnp.int32)
    y_index = jnp.arange(NY, dtype=jnp.int32)
    x_pos = x_index.astype(jnp.float32) * (2.0 * math.pi / NX)
    y_pos = y_index.astype(jnp.float32) * (2.0 * math.pi / NY)
    beam_x = 0.6 + 0.4 * jnp.cos(x_pos + phases[0])
    beam_y = 0.6 + 0.4 * jnp.cos(y_pos + phases[1])
    parity = (x_index[:, None] + y_index[None, :]) % 2
    alternate = jnp.where(parity == 0, 1.0, -1.0).astype(jnp.float32)
    beam = beam_level * alternate * beam_x[:, None] * beam_y[None, :]
    tilted = beam[None, :, :, None] * (tone * time_scale[None, :])[:, None, None, :]
    rough = 0.5 * base * pixel_scale[None, :, :, None] * time_scale[None, None, None, :]
    values = jnp.clip(tilted + rough, -19.5, 19.5)
    return values.astype(jnp.bfloat16)


def block_levels(key, dims, pieces, low, high):
    def one(axis_at, parts):
        steps = jax.random.uniform(jax.random.fold_in(jax.random.fold_in(key, 6), axis_at), (parts,), jnp.float32, low / len(pieces), high / len(pieces))
        return jnp.repeat(jnp.exp(steps), dims[axis_at] // parts).reshape((-1,) + (1,) * (len(dims) - axis_at - 1))

    factor_of = one(*pieces[0])
    for cut in pieces[1:]:
        factor_of = factor_of * one(*cut)
    return factor_of


def setup_inputs(seed: int = 0) -> dict:
    seeds = jax.random.split(jax.random.key(seed), 4)
    field = draw_field(jax.random.fold_in(seeds[3], 71), 0)
    gain = jnp.clip(jnp.exp(math.log(1.0) - 1.609438 * jax.random.uniform(seeds[1], (NX, NY), jnp.float32) ** block_levels(seeds[1], (NX, NY), ((0, 64), (1, 4)), -0.2, 0.2)), 0.2, 1.0)
    spectral_phase = jnp.clip(jax.random.uniform(seeds[2], (NT,), jnp.float32, -3.140625, 3.140625), -3.140625, 3.140625)
    return {"field": field, "gain": gain, "spectral_phase": spectral_phase}


kerr_coeff = 0.25
saturation = 1.0
diffract_coeff = 120.0

def dft_tables(count):
    index = jnp.arange(count, dtype=jnp.int32)
    product = index[:, None] * index[None, :] % count
    angle = product.astype(jnp.float32) * (2.0 * math.pi / count)
    factor = 1.0 / math.sqrt(count)
    return ((jnp.cos(angle) * factor).astype(jnp.bfloat16), (jnp.sin(angle) * factor).astype(jnp.bfloat16))

def along_axis(real_part, imag_part, axis, sign):
    count = real_part.shape[axis]
    cos_table, sin_table = dft_tables(count)
    moved_real = jnp.moveaxis(real_part, axis, -1)
    moved_imag = jnp.moveaxis(imag_part, axis, -1)
    layout = moved_real.shape
    flat_real = moved_real.reshape(-1, count)
    flat_imag = moved_imag.reshape(-1, count)
    cos_real = jnp.dot(flat_real, cos_table, preferred_element_type=jnp.float32)
    sin_imag = jnp.dot(flat_imag, sin_table, preferred_element_type=jnp.float32)
    cos_imag = jnp.dot(flat_imag, cos_table, preferred_element_type=jnp.float32)
    sin_real = jnp.dot(flat_real, sin_table, preferred_element_type=jnp.float32)
    out_real = (cos_real - sign * sin_imag).reshape(layout)
    out_imag = (cos_imag + sign * sin_real).reshape(layout)
    return (jnp.moveaxis(out_real, -1, axis), jnp.moveaxis(out_imag, -1, axis))

def signed_freq(index, count):
    return jnp.where(index < count // 2, index, index - count).astype(jnp.float32) / count

def reference(field, gain, spectral_phase):
    real_part = field[0].astype(jnp.float32)
    imag_part = field[1].astype(jnp.float32)
    intensity = real_part * real_part + imag_part * imag_part
    fluence = lax.optimization_barrier(jnp.mean(intensity, axis=-1, keepdims=True))
    amplitude = jnp.exp(gain[:, :, None] / (1.0 + fluence / saturation))
    kerr_phase = kerr_coeff * intensity
    cos_kerr = jnp.cos(kerr_phase)
    sin_kerr = jnp.sin(kerr_phase)
    kerr_real = (amplitude * (real_part * cos_kerr - imag_part * sin_kerr)).astype(jnp.bfloat16)
    kerr_imag = (amplitude * (real_part * sin_kerr + imag_part * cos_kerr)).astype(jnp.bfloat16)
    spec_real, spec_imag = along_axis(kerr_real, kerr_imag, 2, -1.0)
    spec_real = spec_real.astype(jnp.bfloat16)
    spec_imag = spec_imag.astype(jnp.bfloat16)
    rows_real, rows_imag = along_axis(spec_real, spec_imag, 0, -1.0)
    rows_real = rows_real.astype(jnp.bfloat16)
    rows_imag = rows_imag.astype(jnp.bfloat16)
    plane_real, plane_imag = along_axis(rows_real, rows_imag, 1, -1.0)
    count_x = field.shape[1]
    count_y = field.shape[2]
    count_time = field.shape[3]
    wave_x = signed_freq(jnp.arange(count_x, dtype=jnp.int32), count_x)
    wave_y = signed_freq(jnp.arange(count_y, dtype=jnp.int32), count_y)
    wave_f = signed_freq(jnp.arange(count_time, dtype=jnp.int32), count_time)
    wave = (wave_x * wave_x)[:, None, None] + (wave_y * wave_y)[None, :, None]
    theta = spectral_phase[None, None, :] - diffract_coeff * wave / (1.0 + 0.5 * wave_f)[None, None, :]
    cos_theta = jnp.cos(theta)
    sin_theta = jnp.sin(theta)
    prop_real = (plane_real * cos_theta - plane_imag * sin_theta).astype(jnp.bfloat16)
    prop_imag = (plane_real * sin_theta + plane_imag * cos_theta).astype(jnp.bfloat16)
    back_real, back_imag = along_axis(prop_real, prop_imag, 1, 1.0)
    back_real = back_real.astype(jnp.bfloat16)
    back_imag = back_imag.astype(jnp.bfloat16)
    home_real, home_imag = along_axis(back_real, back_imag, 0, 1.0)
    home_real = home_real.astype(jnp.bfloat16)
    home_imag = home_imag.astype(jnp.bfloat16)
    out_real, out_imag = along_axis(home_real, home_imag, 2, 1.0)
    return jnp.stack([out_real, out_imag]).astype(jnp.bfloat16)
```

```python
import math

import jax
import jax.numpy as jnp
import numpy as np
from jax import lax
from jax.experimental import pallas as pl
from jax.experimental.pallas import tpu as pltpu
from jax.sharding import PartitionSpec as P

MESH = pl.DeviceIdType.MESH
BF16 = jnp.bfloat16
F32 = jnp.float32

N = 512
DEV = 256
WIDE = 64
NARROW = 4
ROWS = 8
COLS = 128
KERR = 0.25
SATURATION = 1.0
DIFFRACT = 120.0
ROW_STRIDE = DEV

def _fit(func, count):
    nodes = 0.125 * (1.0 - np.cos((np.arange(400) + 0.5) * np.pi / 400))
    powers = nodes[:, None] ** np.arange(count)[None, :]
    return [float(v) for v in np.linalg.lstsq(powers, func(np.sqrt(nodes)), rcond=None)[0]]


SIN_TERMS = _fit(lambda z: np.sin(2 * np.pi * z) / z, 7)
COS_TERMS = _fit(lambda z: np.cos(2 * np.pi * z), 7)


def horner(terms, value):
    total = terms[-1]
    for term in terms[-2::-1]:
        total = total * value + term
    return total


def dft_tables(count):
    index = np.arange(count)
    angle = (index[:, None] * index[None, :] % count) * (2.0 * math.pi / count)
    factor = 1.0 / math.sqrt(count)
    return np.cos(angle) * factor, np.sin(angle) * factor


def signed_freq(index, count):
    return np.where(index < count // 2, index, index - count) / count


def time_tables():
    cos_table, sin_table = dft_tables(N)
    forward = np.block([[cos_table, sin_table], [-sin_table, cos_table]])
    inverse = np.block([[cos_table, sin_table], [-sin_table, cos_table]])
    order = np.arange(2 * N).reshape(2, 2, DEV).transpose(1, 0, 2).reshape(-1)
    return forward[order].astype(BF16), inverse[order].astype(BF16)


def line_kernels():
    index = np.arange(N)
    wave = signed_freq(index, N)
    chirp = np.exp(-1j * DIFFRACT * (wave * wave)[None, :] / (1.0 + 0.5 * wave)[:, None])
    lines = np.fft.ifft(chirp, axis=1)
    return np.stack([lines.real, lines.imag], axis=1).reshape(N, 8, 128).astype(np.float32)


def kernel(
    field_hbm,
    gain_ref,
    phase_ref,
    forward_hbm,
    inverse_hbm,
    lines_hbm,
    out_ref,
    field,
    kerr,
    forward,
    inverse,
    lines,
    circ,
    gain_t,
    spread,
    send1,
    recv1,
    plane,
    send2,
    recv2,
    total,
    load_sem,
    send_sem,
    recv_sem,
):
    wide = lax.axis_index("wide")
    narrow = lax.axis_index("narrow")
    me = wide * NARROW + narrow
    place = narrow * WIDE + wide

    barrier = pltpu.get_barrier_semaphore()

    @pl.loop(1, DEV)
    def _(step):
        other = lax.rem(me + step, DEV)
        pl.semaphore_signal(
            barrier, inc=1, device_id=(other // NARROW, lax.rem(other, NARROW)), device_id_type=MESH
        )

    loads = [
        pltpu.make_async_copy(field_hbm, field, load_sem.at[0]),
        pltpu.make_async_copy(forward_hbm, forward, load_sem.at[1]),
        pltpu.make_async_copy(lines_hbm.at[pl.ds(me, 1)], lines.at[pl.ds(0, 1)], load_sem.at[2]),
        pltpu.make_async_copy(lines_hbm.at[pl.ds(DEV + me, 1)], lines.at[pl.ds(1, 1)], load_sem.at[3]),
        pltpu.make_async_copy(inverse_hbm, inverse, load_sem.at[4]),
    ]
    for load in loads:
        load.start()

    gain_t[...] = jnp.transpose(gain_ref[...])
    loads[0].wait()

    block = 32

    @pl.loop(0, ROWS * COLS // block)
    def _(step):
        row = step // (COLS // block)
        col = pl.multiple_of(lax.rem(step, COLS // block) * block, block)
        real = field[0, row, pl.ds(col, block), :].astype(F32)
        imag = field[1, row, pl.ds(col, block), :].astype(F32)
        intensity = real * real + imag * imag
        fluence = jnp.sum(intensity, axis=1, keepdims=True) * (1.0 / N)
        gains = gain_t[pl.ds(col, block), :]
        lane = lax.broadcasted_iota(jnp.int32, gains.shape, 1)
        gain = jnp.sum(jnp.where(lane == row, gains, 0.0), axis=1, keepdims=True)
        amplitude = jnp.exp(gain / (1.0 + fluence / SATURATION))
        turns = intensity * (KERR / (2.0 * math.pi))
        turns = turns - jnp.round(turns)
        square = turns * turns
        sin_kerr = turns * horner(SIN_TERMS, square)
        cos_kerr = horner(COS_TERMS, square)
        at = pl.ds(pl.multiple_of(step * block, block), block)
        kerr[at, :N] = (amplitude * (real * cos_kerr - imag * sin_kerr)).astype(BF16)
        kerr[at, N:] = (amplitude * (real * sin_kerr + imag * cos_kerr)).astype(BF16)

    loads[1].wait()

    def time_forward(part):
        @pl.loop(0, ROWS // 2)
        def _(pair):
            at = pl.ds(pl.multiple_of(pair * 2 * COLS, 2 * COLS), 2 * COLS)
            spectrum = lax.dot_general(
                forward[part * 2 * DEV : (part + 1) * 2 * DEV, :],
                kerr[at, :],
                (((1,), (1,)), ((), ())),
                preferred_element_type=F32,
            )
            for c in range(2):
                for r in range(2):
                    start = pl.multiple_of((c * ROWS + pair * 2 + r) * ROW_STRIDE, DEV)
                    spread[pl.ds(start, DEV), :] = spectrum[
                        c * DEV : (c + 1) * DEV, r * COLS : (r + 1) * COLS
                    ]

    def gather_tile(index):
        parts = [
            spread[pl.ds(c * ROWS * ROW_STRIDE + index, ROWS, stride=ROW_STRIDE), :] for c in range(2)
        ]
        return jnp.concatenate(parts, axis=0).astype(BF16)

    def send_spectrum(part):
        @pl.loop(1, DEV)
        def _(step):
            other = lax.rem(me + step, DEV)
            send1[part, other] = gather_tile(other)
            pltpu.make_async_remote_copy(
                src_ref=send1.at[part, other],
                dst_ref=recv1.at[part, place],
                send_sem=send_sem.at[part],
                recv_sem=recv_sem.at[part],
                device_id=(other // NARROW, lax.rem(other, NARROW)),
                device_id_type=MESH,
            ).start()

        recv1[part, place] = gather_tile(me)

    def make_circulant(part):
        half_phase = 0.5 * phase_ref[part * DEV + me]
        angle = jnp.full((1, N), half_phase, F32)
        cos_half = jnp.cos(angle)
        sin_half = jnp.sin(angle)
        real = jnp.concatenate([lines[part, j : j + 1, :] for j in range(4)], axis=1)
        imag = jnp.concatenate([lines[part, 4 + j : 5 + j, :] for j in range(4)], axis=1)
        turned = (real * cos_half - imag * sin_half, real * sin_half + imag * cos_half)
        for c in range(2):
            first = pltpu.roll(
                jnp.broadcast_to(turned[c], (COLS, N)), 0, 1, stride=1, stride_axis=0
            ).astype(BF16)
            for j in range(4):
                for k in range(4):
                    source = (k - j) % 4
                    circ[part, c, j * COLS : (j + 1) * COLS, k * COLS : (k + 1) * COLS] = first[
                        :, source * COLS : (source + 1) * COLS
                    ]

    def transform_plane(part):
        real_circ = circ[part, 0]
        imag_circ = circ[part, 1]
        group = 16

        @pl.loop(0, WIDE // group)
        def _(step):
            at = pl.multiple_of(step * group, group)
            lines_in = jnp.concatenate(
                [
                    recv1[part, pl.ds(j * WIDE + at, group)].reshape(group * 2 * ROWS, COLS)
                    for j in range(NARROW)
                ],
                axis=1,
            )
            by_real = jnp.dot(lines_in, real_circ, preferred_element_type=F32)
            by_imag = jnp.dot(lines_in, imag_circ, preferred_element_type=F32)
            by_real = by_real.reshape(group, 2, ROWS, N)
            by_imag = by_imag.reshape(group, 2, ROWS, N)
            rows = pl.ds(pl.multiple_of(step * group * ROWS, group * ROWS), group * ROWS)
            real = by_real[:, 0] - by_imag[:, 1]
            imag = by_imag[:, 0] + by_real[:, 1]
            plane[0, rows, :] = real.reshape(group * ROWS, N).astype(BF16)
            plane[1, rows, :] = imag.reshape(group * ROWS, N).astype(BF16)

        for half in range(2):
            cols = slice(half * 2 * COLS, (half + 1) * 2 * COLS)
            real_in = plane[0, :, cols]
            imag_in = plane[1, :, cols]
            real = jnp.dot(real_circ, real_in, preferred_element_type=F32) - jnp.dot(
                imag_circ, imag_in, preferred_element_type=F32
            )
            imag = jnp.dot(imag_circ, real_in, preferred_element_type=F32) + jnp.dot(
                real_circ, imag_in, preferred_element_type=F32
            )
            both = jnp.concatenate(
                [real.reshape(WIDE, ROWS, 2 * COLS), imag.reshape(WIDE, ROWS, 2 * COLS)], axis=1
            ).astype(BF16)
            for j in range(2):
                at = (2 * half + j) * WIDE
                send2[part, at : at + WIDE] = both[:, :, j * COLS : (j + 1) * COLS]

    def send_back(part):
        @pl.loop(1, DEV)
        def _(step):
            other = lax.rem(me + step, DEV)
            other_wide = other // NARROW
            other_narrow = lax.rem(other, NARROW)
            pltpu.make_async_remote_copy(
                src_ref=send2.at[part, other_narrow * WIDE + other_wide],
                dst_ref=recv2.at[part, me],
                send_sem=send_sem.at[2 + part],
                recv_sem=recv_sem.at[2 + part],
                device_id=(other_wide, other_narrow),
                device_id_type=MESH,
            ).start()

        recv2[part, me] = send2[part, place]

    def wait_bytes(buffer, part, sem):
        view = buffer.at[part, pl.ds(0, DEV - 1)]
        pltpu.make_async_copy(view, view, sem).wait()

    def time_inverse(part):
        @pl.loop(0, DEV, unroll=8)
        def _(index):
            tile = recv2[part, index].astype(F32)
            for c in range(2):
                spread[pl.ds(c * ROWS * ROW_STRIDE + index, ROWS, stride=ROW_STRIDE), :] = tile[
                    c * ROWS : (c + 1) * ROWS
                ]

        @pl.loop(0, ROWS // 2)
        def _(pair):
            columns = []
            for r in range(2):
                pieces = []
                for c in range(2):
                    start = pl.multiple_of((c * ROWS + pair * 2 + r) * ROW_STRIDE, DEV)
                    pieces.append(spread[pl.ds(start, DEV), :])
                columns.append(jnp.concatenate(pieces, axis=0))
            spectrum = jnp.concatenate(columns, axis=1).astype(BF16)
            result = lax.dot_general(
                spectrum,
                inverse[part * 2 * DEV : (part + 1) * 2 * DEV, :],
                (((0,), (0,)), ((), ())),
                preferred_element_type=F32,
            )
            at = pl.ds(pl.multiple_of(pair * 2 * COLS, 2 * COLS), 2 * COLS)
            if part == 0:
                total[at, :] = result
            else:
                result = result + total[at, :]
                for r in range(2):
                    for c in range(2):
                        out_ref[c, pair * 2 + r] = result[
                            r * COLS : (r + 1) * COLS, c * N : (c + 1) * N
                        ].astype(BF16)

    time_forward(0)
    pl.semaphore_wait(barrier, DEV - 1)
    send_spectrum(0)
    time_forward(1)
    send_spectrum(1)
    loads[2].wait()
    loads[3].wait()
    loads[4].wait()
    for part in range(2):
        make_circulant(part)
    for part in range(2):
        wait_bytes(recv1, part, recv_sem.at[part])
        transform_plane(part)
        send_back(part)
    for part in range(2):
        wait_bytes(recv2, part, recv_sem.at[2 + part])
        time_inverse(part)
    for part in range(2):
        wait_bytes(send1, part, send_sem.at[part])
        wait_bytes(send2, part, send_sem.at[2 + part])


def local(field, gain, spectral_phase):
    forward, inverse = time_tables()
    any_spec = pl.BlockSpec(memory_space=pl.ANY)
    return pl.pallas_call(
        kernel,
        out_shape=jax.ShapeDtypeStruct((2, ROWS, COLS, N), BF16),
        in_specs=[
            any_spec,
            pl.BlockSpec(memory_space=pltpu.VMEM),
            pl.BlockSpec(memory_space=pltpu.SMEM),
            any_spec,
            any_spec,
            any_spec,
        ],
        out_specs=pl.BlockSpec(memory_space=pltpu.VMEM),
        scratch_shapes=[
            pltpu.VMEM((2, ROWS, COLS, N), BF16),
            pltpu.VMEM((ROWS * COLS, 2 * N), BF16),
            pltpu.VMEM((2 * N, 2 * N), BF16),
            pltpu.VMEM((2 * N, 2 * N), BF16),
            pltpu.VMEM((2, 8, 128), F32),
            pltpu.VMEM((2, 2, N, N), BF16),
            pltpu.VMEM((COLS, ROWS), F32),
            pltpu.VMEM((2 * ROWS * ROW_STRIDE, COLS), F32),
            pltpu.VMEM((2, DEV, 2 * ROWS, COLS), BF16),
            pltpu.VMEM((2, DEV, 2 * ROWS, COLS), BF16),
            pltpu.VMEM((2, N, N), BF16),
            pltpu.VMEM((2, DEV, 2 * ROWS, COLS), BF16),
            pltpu.VMEM((2, DEV, 2 * ROWS, COLS), BF16),
            pltpu.VMEM((ROWS * COLS, 2 * N), F32),
            pltpu.SemaphoreType.DMA((5,)),
            pltpu.SemaphoreType.DMA((4,)),
            pltpu.SemaphoreType.DMA((4,)),
        ],
        compiler_params=pltpu.CompilerParams(
            collective_id=0, has_side_effects=True, vmem_limit_bytes=56 << 20
        ),
    )(
        field,
        gain,
        spectral_phase,
        jnp.asarray(forward),
        jnp.asarray(inverse),
        jnp.asarray(line_kernels()),
    )


def solution(mesh):
    in_specs = (P(None, "wide", "narrow", None), P("wide", "narrow"), P())
    out_specs = P(None, "wide", "narrow", None)
    return jax.shard_map(local, mesh=mesh, in_specs=in_specs, out_specs=out_specs, check_vma=False)
```

```python
import math

import jax
import jax.numpy as jnp
import numpy as np
from jax import lax
from jax.experimental import pallas as pl
from jax.experimental.pallas import tpu as pltpu
from jax.sharding import PartitionSpec as P

MESH = pl.DeviceIdType.MESH
BF16 = jnp.bfloat16
F32 = jnp.float32

N = 512
DEV = 256
HALF = N // 2
WIDE = 64
NARROW = 4
ROWS = 8
COLS = 128
KERR = 0.25
SATURATION = 1.0
DIFFRACT = 120.0
ROW_STRIDE = DEV + 8

def _fit(func, count):
    nodes = 0.125 * (1.0 - np.cos((np.arange(400) + 0.5) * np.pi / 400))
    powers = nodes[:, None] ** np.arange(count)[None, :]
    return [float(v) for v in np.linalg.lstsq(powers, func(np.sqrt(nodes)), rcond=None)[0]]


SIN_TERMS = _fit(lambda z: np.sin(2 * np.pi * z) / z, 6)
COS_TERMS = _fit(lambda z: np.cos(2 * np.pi * z), 6)


def horner(terms, value):
    total = terms[-1]
    for term in terms[-2::-1]:
        total = total * value + term
    return total


def dft_tables(count):
    index = np.arange(count)
    angle = (index[:, None] * index[None, :] % count) * (2.0 * math.pi / count)
    factor = 1.0 / math.sqrt(count)
    return np.cos(angle) * factor, np.sin(angle) * factor


def signed_freq(index, count):
    return np.where(index < count // 2, index, index - count) / count


def time_tables():
    cos_table, sin_table = dft_tables(N)
    tables = []
    for part in range(2):
        cos_part = cos_table[part::2, :HALF]
        sin_part = sin_table[part::2, :HALF]
        tables.append(np.block([[cos_part, sin_part], [-sin_part, cos_part]]))
    return np.stack(tables).astype(BF16)


def line_kernels():
    index = np.arange(N)
    wave = signed_freq(index, N)
    chirp = np.exp(-1j * DIFFRACT * (wave * wave)[None, :] / (1.0 + 0.5 * wave)[:, None])
    lines = np.fft.ifft(chirp, axis=1)
    return np.stack([lines.real, lines.imag], axis=1).reshape(N, 8, 128).astype(np.float32)


def kernel(
    field_hbm,
    gain_ref,
    phase_ref,
    table_hbm,
    lines_hbm,
    real_hbm,
    imag_hbm,
    field,
    kerr,
    table,
    lines,
    circ,
    gain_t,
    spread,
    send1,
    recv1,
    plane,
    send2,
    recv2,
    total,
    load_sem,
    send_sem,
    recv_sem,
    store_sem,
):
    wide = lax.axis_index("wide")
    narrow = lax.axis_index("narrow")
    me = wide * NARROW + narrow
    place = narrow * WIDE + wide

    barrier = pltpu.get_barrier_semaphore()

    fields = []
    for pair in range(ROWS // 2):
        at = pl.ds(2 * pair, 2)
        fields.append(pltpu.make_async_copy(field_hbm.at[:, at], field.at[:, at], load_sem.at[pair]))
    loads = [
        pltpu.make_async_copy(table_hbm, table, load_sem.at[4]),
        pltpu.make_async_copy(lines_hbm.at[pl.ds(2 * me, 2)], lines, load_sem.at[5]),
    ]
    for load in fields + loads:
        load.start()

    @pl.loop(1, DEV)
    def _(step):
        other = lax.rem(me + step, DEV)
        pl.semaphore_signal(
            barrier, inc=1, device_id=(other // NARROW, lax.rem(other, NARROW)), device_id_type=MESH
        )

    gain_t[...] = jnp.transpose(gain_ref[...])
    block = 32

    def kerr_pair(pair):
        @pl.loop(0, 2 * COLS // block)
        def _(step):
            row = 2 * pair + step // (COLS // block)
            col = pl.multiple_of(lax.rem(step, COLS // block) * block, block)
            real = field[0, row, pl.ds(col, block), :].astype(F32)
            imag = field[1, row, pl.ds(col, block), :].astype(F32)
            intensity = real * real + imag * imag
            fluence = jnp.sum(intensity, axis=1, keepdims=True) * (1.0 / N)
            gains = gain_t[pl.ds(col, block), :]
            lane = lax.broadcasted_iota(jnp.int32, gains.shape, 1)
            gain = jnp.sum(jnp.where(lane == row, gains, 0.0), axis=1, keepdims=True)
            amplitude = jnp.exp(gain / (1.0 + fluence / SATURATION))
            turns = intensity * (KERR / (2.0 * math.pi))
            turns = turns - jnp.round(turns)
            square = turns * turns
            sin_kerr = amplitude * turns * horner(SIN_TERMS, square)
            cos_kerr = amplitude * horner(COS_TERMS, square)
            kerr_real = real * cos_kerr - imag * sin_kerr
            kerr_imag = real * sin_kerr + imag * cos_kerr
            at = pl.ds(pl.multiple_of(pair * 2 * COLS + step * block, block), block)
            for c, value in enumerate((kerr_real, kerr_imag)):
                first = value[:, :HALF]
                second = value[:, HALF:]
                kerr[0, at, c * HALF : (c + 1) * HALF] = (first + second).astype(BF16)
                kerr[1, at, c * HALF : (c + 1) * HALF] = (first - second).astype(BF16)

    def time_forward(part, pair):
        at = pl.ds(pl.multiple_of(pair * 2 * COLS, 2 * COLS), 2 * COLS)
        spectrum = lax.dot_general(
            table[part], kerr[part, at, :], (((1,), (1,)), ((), ())), preferred_element_type=F32
        )
        for c in range(2):
            for r in range(2):
                start = pl.multiple_of((c * ROWS + pair * 2 + r) * ROW_STRIDE, 8)
                spread[pl.ds(start, DEV), :] = spectrum[
                    c * DEV : (c + 1) * DEV, r * COLS : (r + 1) * COLS
                ]

    def gather_tile(index):
        parts = [
            spread[pl.ds(c * ROWS * ROW_STRIDE + index, ROWS, stride=ROW_STRIDE), :] for c in range(2)
        ]
        return jnp.concatenate(parts, axis=0).astype(BF16)

    def send_spectrum(part):
        @pl.loop(1, DEV)
        def _(step):
            other = lax.rem(me + step, DEV)
            send1[part, other] = gather_tile(other)
            pltpu.make_async_remote_copy(
                src_ref=send1.at[part, other],
                dst_ref=recv1.at[part, place],
                send_sem=send_sem.at[part],
                recv_sem=recv_sem.at[part],
                device_id=(other // NARROW, lax.rem(other, NARROW)),
                device_id_type=MESH,
            ).start()

        recv1[part, place] = gather_tile(me)

    def make_circulant(part):
        half_phase = 0.5 * phase_ref[2 * me + part]
        angle = jnp.full((1, N), half_phase, F32)
        cos_half = jnp.cos(angle)
        sin_half = jnp.sin(angle)
        real = jnp.concatenate([lines[part, j : j + 1, :] for j in range(4)], axis=1)
        imag = jnp.concatenate([lines[part, 4 + j : 5 + j, :] for j in range(4)], axis=1)
        turned = (real * cos_half - imag * sin_half, real * sin_half + imag * cos_half)
        for c in range(2):
            first = pltpu.roll(
                jnp.broadcast_to(turned[c], (COLS, N)), 0, 1, stride=1, stride_axis=0
            ).astype(BF16)
            for j in range(4):
                for k in range(4):
                    source = (k - j) % 4
                    circ[part, c, j * COLS : (j + 1) * COLS, k * COLS : (k + 1) * COLS] = first[
                        :, source * COLS : (source + 1) * COLS
                    ]

    def transform_plane(part):
        real_circ = circ[part, 0]
        imag_circ = circ[part, 1]
        group = 16

        @pl.loop(0, WIDE // group)
        def _(step):
            at = pl.multiple_of(step * group, group)
            lines_in = jnp.concatenate(
                [
                    recv1[part, pl.ds(j * WIDE + at, group)].reshape(group * 2 * ROWS, COLS)
                    for j in range(NARROW)
                ],
                axis=1,
            )
            by_real = jnp.dot(lines_in, real_circ, preferred_element_type=F32)
            by_imag = jnp.dot(lines_in, imag_circ, preferred_element_type=F32)
            by_real = by_real.reshape(group, 2, ROWS, N)
            by_imag = by_imag.reshape(group, 2, ROWS, N)
            rows = pl.ds(pl.multiple_of(step * group * ROWS, group * ROWS), group * ROWS)
            real = by_real[:, 0] - by_imag[:, 1]
            imag = by_imag[:, 0] + by_real[:, 1]
            plane[0, rows, :] = real.reshape(group * ROWS, N).astype(BF16)
            plane[1, rows, :] = imag.reshape(group * ROWS, N).astype(BF16)

        for half in range(2):
            cols = slice(half * 2 * COLS, (half + 1) * 2 * COLS)
            real_in = plane[0, :, cols]
            imag_in = plane[1, :, cols]
            real = jnp.dot(real_circ, real_in, preferred_element_type=F32) - jnp.dot(
                imag_circ, imag_in, preferred_element_type=F32
            )
            imag = jnp.dot(imag_circ, real_in, preferred_element_type=F32) + jnp.dot(
                real_circ, imag_in, preferred_element_type=F32
            )
            both = jnp.concatenate(
                [real.reshape(WIDE, ROWS, 2 * COLS), imag.reshape(WIDE, ROWS, 2 * COLS)], axis=1
            ).astype(BF16)
            for j in range(2):
                at = (2 * half + j) * WIDE
                send2[part, at : at + WIDE] = both[:, :, j * COLS : (j + 1) * COLS]

    def send_back(part):
        @pl.loop(1, DEV)
        def _(step):
            other = lax.rem(me + step, DEV)
            other_wide = other // NARROW
            other_narrow = lax.rem(other, NARROW)
            pltpu.make_async_remote_copy(
                src_ref=send2.at[part, other_narrow * WIDE + other_wide],
                dst_ref=recv2.at[part, me],
                send_sem=send_sem.at[2 + part],
                recv_sem=recv_sem.at[2 + part],
                device_id=(other_wide, other_narrow),
                device_id_type=MESH,
            ).start()

        recv2[part, me] = send2[part, place]

    def wait_bytes(buffer, part, sem):
        view = buffer.at[part, pl.ds(0, DEV - 1)]
        pltpu.make_async_copy(view, view, sem).wait()

    def stores(pair):
        at = pl.ds(pair * 2, 2)
        return [
            pltpu.make_async_copy(field.at[c, at], out.at[at], store_sem.at[pair, c])
            for c, out in enumerate((real_hbm, imag_hbm))
        ]

    def time_inverse(part):
        @pl.loop(0, DEV, unroll=8)
        def _(index):
            tile = recv2[part, index].astype(F32)
            for c in range(2):
                spread[pl.ds(c * ROWS * ROW_STRIDE + index, ROWS, stride=ROW_STRIDE), :] = tile[
                    c * ROWS : (c + 1) * ROWS
                ]

        @pl.loop(0, ROWS // 2)
        def _(pair):
            columns = []
            for r in range(2):
                pieces = []
                for c in range(2):
                    start = pl.multiple_of((c * ROWS + pair * 2 + r) * ROW_STRIDE, 8)
                    pieces.append(spread[pl.ds(start, DEV), :])
                columns.append(jnp.concatenate(pieces, axis=0))
            spectrum = jnp.concatenate(columns, axis=1).astype(BF16)
            result = lax.dot_general(
                spectrum,
                table[part],
                (((0,), (0,)), ((), ())),
                preferred_element_type=F32,
            )
            at = pl.ds(pl.multiple_of(pair * 2 * COLS, 2 * COLS), 2 * COLS)
            if part == 0:
                total[at, :] = result
            else:
                even = total[at, :]
                for half, value in enumerate((even + result, even - result)):
                    value = value.astype(BF16)
                    for r in range(2):
                        for c in range(2):
                            field[c, pair * 2 + r, :, half * HALF : (half + 1) * HALF] = value[
                                r * COLS : (r + 1) * COLS, c * HALF : (c + 1) * HALF
                            ]
                for store in stores(pair):
                    store.start()

    for pair in range(ROWS // 2):
        fields[pair].wait()
        kerr_pair(pair)
        if pair == 0:
            loads[0].wait()
        time_forward(0, pair)

    pl.semaphore_wait(barrier, DEV - 1)
    send_spectrum(0)

    @pl.loop(0, ROWS // 2)
    def _(pair):
        time_forward(1, pair)

    send_spectrum(1)
    loads[1].wait()
    for part in range(2):
        make_circulant(part)
    for part in range(2):
        wait_bytes(recv1, part, recv_sem.at[part])
        transform_plane(part)
        send_back(part)
    for part in range(2):
        wait_bytes(recv2, part, recv_sem.at[2 + part])
        time_inverse(part)
    for pair in range(ROWS // 2):
        for store in stores(pair):
            store.wait()
    for part in range(2):
        wait_bytes(send1, part, send_sem.at[part])
        wait_bytes(send2, part, send_sem.at[2 + part])


def gather_parts(real_hbm, imag_hbm, out_hbm, held, load_sem, store_sem):
    pieces = [(c, row) for row in range(ROWS) for c in range(2)]
    loads = [
        pltpu.make_async_copy((real_hbm, imag_hbm)[c].at[row], held.at[c, row], load_sem.at[c, row])
        for c, row in pieces
    ]
    stores = [
        pltpu.make_async_copy(held.at[c, row], out_hbm.at[c, row], store_sem.at[c, row])
        for c, row in pieces
    ]
    for load in loads:
        load.start()
    for load, store in zip(loads, stores):
        load.wait()
        store.start()
    for store in stores:
        store.wait()


def local(field, gain, spectral_phase):
    hbm_spec = pl.BlockSpec(memory_space=pltpu.HBM)
    real, imag = pl.pallas_call(
        kernel,
        out_shape=[jax.ShapeDtypeStruct((ROWS, COLS, N), BF16)] * 2,
        in_specs=[
            hbm_spec,
            pl.BlockSpec(memory_space=pltpu.VMEM),
            pl.BlockSpec(memory_space=pltpu.SMEM),
            hbm_spec,
            hbm_spec,
        ],
        out_specs=[hbm_spec] * 2,
        scratch_shapes=[
            pltpu.VMEM((2, ROWS, COLS, N), BF16),
            pltpu.VMEM((2, ROWS * COLS, N), BF16),
            pltpu.VMEM((2, N, N), BF16),
            pltpu.VMEM((2, 8, 128), F32),
            pltpu.VMEM((2, 2, N, N), BF16),
            pltpu.VMEM((COLS, ROWS), F32),
            pltpu.VMEM((2 * ROWS * ROW_STRIDE, COLS), F32),
            pltpu.VMEM((2, DEV, 2 * ROWS, COLS), BF16),
            pltpu.VMEM((2, DEV, 2 * ROWS, COLS), BF16),
            pltpu.VMEM((2, N, N), BF16),
            pltpu.VMEM((2, DEV, 2 * ROWS, COLS), BF16),
            pltpu.VMEM((2, DEV, 2 * ROWS, COLS), BF16),
            pltpu.VMEM((ROWS * COLS, N), F32),
            pltpu.SemaphoreType.DMA((6,)),
            pltpu.SemaphoreType.DMA((4,)),
            pltpu.SemaphoreType.DMA((4,)),
            pltpu.SemaphoreType.DMA((ROWS // 2, 2)),
        ],
        compiler_params=pltpu.CompilerParams(
            collective_id=0, has_side_effects=True, vmem_limit_bytes=56 << 20
        ),
    )(
        field,
        gain,
        spectral_phase,
        jnp.asarray(time_tables()),
        jnp.asarray(line_kernels()),
    )
    return pl.pallas_call(
        gather_parts,
        out_shape=jax.ShapeDtypeStruct((2, ROWS, COLS, N), BF16),
        in_specs=[hbm_spec] * 2,
        out_specs=hbm_spec,
        scratch_shapes=[
            pltpu.VMEM((2, ROWS, COLS, N), BF16),
            pltpu.SemaphoreType.DMA((2, ROWS)),
            pltpu.SemaphoreType.DMA((2, ROWS)),
        ],
        compiler_params=pltpu.CompilerParams(vmem_limit_bytes=56 << 20),
    )(real, imag)


def solution(mesh):
    in_specs = (P(None, "wide", "narrow", None), P("wide", "narrow"), P())
    out_specs = P(None, "wide", "narrow", None)
    return jax.shard_map(local, mesh=mesh, in_specs=in_specs, out_specs=out_specs, check_vma=False)
```

```python
import math

import jax
import jax.numpy as jnp
import numpy as np
from jax import lax
from jax.experimental import pallas as pl
from jax.experimental.pallas import tpu as pltpu
from jax.sharding import PartitionSpec as P

MESH = pl.DeviceIdType.MESH
BF16 = jnp.bfloat16
F32 = jnp.float32

N = 512
DEV = 256
HALF = N // 2
WIDE = 64
NARROW = 4
ROWS = 8
COLS = 128
KERR = 0.25
SATURATION = 1.0
DIFFRACT = 120.0
SEND_UNROLL = 1
ROW_STRIDE = DEV + 8

def _fit(func, count):
    nodes = 0.125 * (1.0 - np.cos((np.arange(400) + 0.5) * np.pi / 400))
    powers = nodes[:, None] ** np.arange(count)[None, :]
    return [float(v) for v in np.linalg.lstsq(powers, func(np.sqrt(nodes)), rcond=None)[0]]


SIN_TERMS = _fit(lambda z: np.sin(2 * np.pi * z) / z, 6)
COS_TERMS = _fit(lambda z: np.cos(2 * np.pi * z), 6)


def horner(terms, value):
    total = terms[-1]
    for term in terms[-2::-1]:
        total = total * value + term
    return total


def dft_tables(count):
    index = np.arange(count)
    angle = (index[:, None] * index[None, :] % count) * (2.0 * math.pi / count)
    factor = 1.0 / math.sqrt(count)
    return np.cos(angle) * factor, np.sin(angle) * factor


def signed_freq(index, count):
    return np.where(index < count // 2, index, index - count) / count


def time_tables():
    cos_table, sin_table = dft_tables(N)
    tables = []
    for part in range(2):
        cos_part = cos_table[part::2, :HALF]
        sin_part = sin_table[part::2, :HALF]
        tables.append(np.block([[cos_part, sin_part], [-sin_part, cos_part]]))
    return np.stack(tables).astype(BF16)


def line_kernels():
    index = np.arange(N)
    wave = signed_freq(index, N)
    chirp = np.exp(-1j * DIFFRACT * (wave * wave)[None, :] / (1.0 + 0.5 * wave)[:, None])
    lines = np.fft.ifft(chirp, axis=1)
    return np.stack([lines.real, lines.imag], axis=1).reshape(N, 8, 128).astype(np.float32)


def kernel(
    field_hbm,
    gain_hbm,
    phase_hbm,
    table_hbm,
    lines_hbm,
    real_hbm,
    imag_hbm,
    field,
    kerr,
    table,
    lines,
    circ,
    gain_ref,
    phase_ref,
    gain_t,
    spread,
    send1,
    recv1,
    plane,
    send2,
    recv2,
    even,
    odd,
    load_sem,
    send_sem,
    recv_sem,
    store_sem,
):
    wide = lax.axis_index("wide")
    narrow = lax.axis_index("narrow")
    me = wide * NARROW + narrow
    place = narrow * WIDE + wide

    barrier = pltpu.get_barrier_semaphore()

    fields = []
    for pair in range(ROWS // 2):
        at = pl.ds(2 * pair, 2)
        fields.append(pltpu.make_async_copy(field_hbm.at[:, at], field.at[:, at], load_sem.at[pair]))
    loads = [
        pltpu.make_async_copy(table_hbm, table, load_sem.at[4]),
        pltpu.make_async_copy(lines_hbm.at[pl.ds(2 * place, 2)], lines, load_sem.at[5]),
        pltpu.make_async_copy(phase_hbm, phase_ref, load_sem.at[7]),
    ]
    load_gain = pltpu.make_async_copy(gain_hbm, gain_ref, load_sem.at[6])
    for load in [load_gain] + fields + loads:
        load.start()

    @pl.loop(1, DEV)
    def _(step):
        other = lax.rem(me + step, DEV)
        pl.semaphore_signal(
            barrier, inc=1, device_id=(other // NARROW, lax.rem(other, NARROW)), device_id_type=MESH
        )

    load_gain.wait()
    gain_t[...] = jnp.transpose(gain_ref[...])
    block = 32

    def kerr_pair(pair):
        @pl.loop(0, 2 * COLS // block, unroll=4)
        def _(step):
            row = 2 * pair + step // (COLS // block)
            col = pl.multiple_of(lax.rem(step, COLS // block) * block, block)
            real = field[0, row, pl.ds(col, block), :].astype(F32)
            imag = field[1, row, pl.ds(col, block), :].astype(F32)
            intensity = real * real + imag * imag
            fluence = jnp.sum(intensity, axis=1, keepdims=True) * (1.0 / N)
            gains = gain_t[pl.ds(col, block), :]
            lane = lax.broadcasted_iota(jnp.int32, gains.shape, 1)
            gain = jnp.sum(jnp.where(lane == row, gains, 0.0), axis=1, keepdims=True)
            amplitude = jnp.exp(gain / (1.0 + fluence / SATURATION))
            turns = intensity * (KERR / (2.0 * math.pi))
            turns = turns - jnp.round(turns)
            square = turns * turns
            sin_kerr = amplitude * turns * horner(SIN_TERMS, square)
            cos_kerr = amplitude * horner(COS_TERMS, square)
            kerr_real = real * cos_kerr - imag * sin_kerr
            kerr_imag = real * sin_kerr + imag * cos_kerr
            at = pl.ds(pl.multiple_of(pair * 2 * COLS + step * block, block), block)
            for c, value in enumerate((kerr_real, kerr_imag)):
                first = value[:, :HALF]
                second = value[:, HALF:]
                kerr[0, at, c * HALF : (c + 1) * HALF] = (first + second).astype(BF16)
                kerr[1, at, c * HALF : (c + 1) * HALF] = (first - second).astype(BF16)

    def pair_rows(pair):
        return pl.ds(pl.multiple_of(pair * 2 * COLS, 2 * COLS), 2 * COLS)

    def time_forward(part, pair):
        at = pair_rows(pair)
        spectrum = lax.dot_general(
            table[part], kerr[part, at, :], (((1,), (1,)), ((), ())), preferred_element_type=F32
        )
        for c in range(2):
            for r in range(2):
                start = pl.multiple_of((c * ROWS + pair * 2 + r) * ROW_STRIDE, 8)
                spread[pl.ds(start, DEV), :] = spectrum[
                    c * DEV : (c + 1) * DEV, r * COLS : (r + 1) * COLS
                ]

    def gather_tile(index):
        parts = [
            spread[pl.ds(c * ROWS * ROW_STRIDE + index, ROWS, stride=ROW_STRIDE), :] for c in range(2)
        ]
        return jnp.concatenate(parts, axis=0).astype(BF16)

    def partner(step):
        other_wide = lax.rem(wide + step, WIDE)
        turn = step // WIDE
        other_chip = lax.rem(narrow // 2 + turn // 2, 2)
        other_core = lax.rem(narrow + turn, 2)
        other_narrow = other_chip * 2 + other_core
        return other_wide, other_narrow, other_narrow * WIDE + other_wide

    def partner_low_first(step):
        turn = lax.rem(step, WIDE)
        core_turn, turn = turn // 32, lax.rem(turn, 32)
        z_turn, turn = turn // 8, lax.rem(turn, 8)
        other_x = lax.rem(wide // 32 + turn // 4, 2)
        other_z = lax.rem(wide // 4 + z_turn, 4) + step // WIDE * 4
        other_y = lax.rem(wide + turn, 4)
        other_wide = other_x * 32 + other_z * 4 + other_y
        other_narrow = lax.rem(narrow // 2 + 1, 2) * 2 + lax.rem(narrow + core_turn, 2)
        return other_wide, other_narrow, other_narrow * WIDE + other_wide

    def send_spectrum(part):
        @pl.loop(1, DEV, unroll=SEND_UNROLL)
        def _(step):
            other_wide, other_narrow, other = partner(step)
            send1[part, other] = gather_tile(other)
            pltpu.make_async_remote_copy(
                src_ref=send1.at[part, other],
                dst_ref=recv1.at[part, place],
                send_sem=send_sem.at[part],
                recv_sem=recv_sem.at[part],
                device_id=(other_wide, other_narrow),
                device_id_type=MESH,
            ).start()

        recv1[part, place] = gather_tile(place)

    def make_circulant(part):
        half_phase = 0.5 * phase_ref[2 * place + part]
        angle = jnp.full((1, N), half_phase, F32)
        cos_half = jnp.cos(angle)
        sin_half = jnp.sin(angle)
        real = jnp.concatenate([lines[part, j : j + 1, :] for j in range(4)], axis=1)
        imag = jnp.concatenate([lines[part, 4 + j : 5 + j, :] for j in range(4)], axis=1)
        turned = (real * cos_half - imag * sin_half, real * sin_half + imag * cos_half)
        for c in range(2):
            first = pltpu.roll(
                jnp.broadcast_to(turned[c], (COLS, N)), 0, 1, stride=1, stride_axis=0
            ).astype(BF16)
            for j in range(4):
                for k in range(4):
                    source = (k - j) % 4
                    circ[part, c, j * COLS : (j + 1) * COLS, k * COLS : (k + 1) * COLS] = first[
                        :, source * COLS : (source + 1) * COLS
                    ]

    def transform_plane(part):
        real_circ = circ[part, 0]
        imag_circ = circ[part, 1]
        group = 16

        @pl.loop(0, WIDE // group)
        def _(step):
            at = pl.multiple_of(step * group, group)
            lines_in = jnp.concatenate(
                [
                    recv1[part, pl.ds(j * WIDE + at, group)].reshape(group * 2 * ROWS, COLS)
                    for j in range(NARROW)
                ],
                axis=1,
            )
            by_real = jnp.dot(lines_in, real_circ, preferred_element_type=F32)
            by_imag = jnp.dot(lines_in, imag_circ, preferred_element_type=F32)
            by_real = by_real.reshape(group, 2, ROWS, N)
            by_imag = by_imag.reshape(group, 2, ROWS, N)
            rows = pl.ds(pl.multiple_of(step * group * ROWS, group * ROWS), group * ROWS)
            real = by_real[:, 0] - by_imag[:, 1]
            imag = by_imag[:, 0] + by_real[:, 1]
            plane[0, rows, :] = real.reshape(group * ROWS, N).astype(BF16)
            plane[1, rows, :] = imag.reshape(group * ROWS, N).astype(BF16)

        for half in range(2):
            cols = slice(half * 2 * COLS, (half + 1) * 2 * COLS)
            real_in = plane[0, :, cols]
            imag_in = plane[1, :, cols]
            real = jnp.dot(real_circ, real_in, preferred_element_type=F32) - jnp.dot(
                imag_circ, imag_in, preferred_element_type=F32
            )
            imag = jnp.dot(imag_circ, real_in, preferred_element_type=F32) + jnp.dot(
                real_circ, imag_in, preferred_element_type=F32
            )
            both = jnp.concatenate(
                [real.reshape(WIDE, ROWS, 2 * COLS), imag.reshape(WIDE, ROWS, 2 * COLS)], axis=1
            ).astype(BF16)
            for j in range(2):
                at = (2 * half + j) * WIDE
                send2[part, at : at + WIDE] = both[:, :, j * COLS : (j + 1) * COLS]

    def send_back(part):
        for half in range(2):

            @pl.loop(max(1, half * DEV // 2), (half + 1) * DEV // 2, unroll=SEND_UNROLL)
            def _(step):
                if part == 1 and half == 1:
                    other_wide, other_narrow, other = partner_low_first(step - DEV // 2)
                else:
                    other_wide, other_narrow, other = partner(step)
                pltpu.make_async_remote_copy(
                    src_ref=send2.at[part, other],
                    dst_ref=recv2.at[part, place],
                    send_sem=send_sem.at[2 + part],
                    recv_sem=recv_sem.at[2 + 2 * part + half],
                    device_id=(other_wide, other_narrow),
                    device_id_type=MESH,
                ).start()

        recv2[part, place] = send2[part, place]

    def wait_bytes(buffer, part, sem, count=DEV - 1):
        view = buffer.at[part, pl.ds(0, count)]
        pltpu.make_async_copy(view, view, sem).wait()

    def stores(pair):
        at = pl.ds(pair * 2, 2)
        return [
            pltpu.make_async_copy(field.at[c, at], out.at[at], store_sem.at[pair, c])
            for c, out in enumerate((real_hbm, imag_hbm))
        ]

    def unpack(part, start, count):
        @pl.loop(0, count, unroll=8)
        def _(step):
            index = start + step
            tile = recv2[part, index].astype(F32)
            for c in range(2):
                spread[pl.ds(c * ROWS * ROW_STRIDE + index, ROWS, stride=ROW_STRIDE), :] = tile[
                    c * ROWS : (c + 1) * ROWS
                ]

    def time_inverse(part, pair, start, count):
        columns = []
        for r in range(2):
            pieces = []
            for c in range(2):
                base = pl.multiple_of((c * ROWS + pair * 2 + r) * ROW_STRIDE + start, 8)
                pieces.append(spread[pl.ds(base, count), :])
            columns.append(jnp.concatenate(pieces, axis=0))
        spectrum = jnp.concatenate(columns, axis=1).astype(BF16)
        rows = [table[part, pl.ds(pl.multiple_of(c * DEV + start, WIDE), count), :] for c in range(2)]
        return lax.dot_general(
            spectrum,
            jnp.concatenate(rows, axis=0),
            (((0,), (0,)), ((), ())),
            preferred_element_type=F32,
        )

    def inverse_even():
        unpack(0, 0, DEV)

        @pl.loop(0, ROWS // 2)
        def _(pair):
            even[pair_rows(pair), :] = time_inverse(0, pair, 0, DEV)

    def inverse_odd(half):
        start = pl.multiple_of(lax.rem(narrow // 2 + half, 2) * 2 * WIDE, 2 * WIDE)
        unpack(1, start, 2 * WIDE)

        @pl.loop(0, ROWS // 2)
        def _(pair):
            at = pair_rows(pair)
            result = time_inverse(1, pair, start, 2 * WIDE)
            if half == 0:
                odd[at, :] = result
                return
            result = result + odd[at, :]
            first = even[at, :]
            for j, value in enumerate((first + result, first - result)):
                value = value.astype(BF16)
                for r in range(2):
                    for c in range(2):
                        field[c, pair * 2 + r, :, j * HALF : (j + 1) * HALF] = value[
                            r * COLS : (r + 1) * COLS, c * HALF : (c + 1) * HALF
                        ]
            for store in stores(pair):
                store.start()

    for pair in range(ROWS // 2):
        fields[pair].wait()
        kerr_pair(pair)
        if pair == 0:
            loads[0].wait()
        time_forward(0, pair)

    pl.semaphore_wait(barrier, DEV - 1)
    send_spectrum(0)

    @pl.loop(0, ROWS // 2)
    def _(pair):
        time_forward(1, pair)

    send_spectrum(1)
    loads[1].wait()
    loads[2].wait()
    for part in range(2):
        make_circulant(part)
    for part in range(2):
        wait_bytes(recv1, part, recv_sem.at[part])
        transform_plane(part)
        send_back(part)
    wait_bytes(recv2, 0, recv_sem.at[2], DEV // 2 - 1)
    wait_bytes(recv2, 0, recv_sem.at[3], DEV // 2)
    inverse_even()
    wait_bytes(recv2, 1, recv_sem.at[4], DEV // 2 - 1)
    inverse_odd(0)
    wait_bytes(recv2, 1, recv_sem.at[5], DEV // 2)
    inverse_odd(1)
    for pair in range(ROWS // 2):
        for store in stores(pair):
            store.wait()
    for part in range(2):
        wait_bytes(send1, part, send_sem.at[part])
        wait_bytes(send2, part, send_sem.at[2 + part])


def gather_parts(real_hbm, imag_hbm, out_hbm, held, load_sem, store_sem):
    pieces = [(c, row) for row in range(ROWS) for c in range(2)]
    loads = [
        pltpu.make_async_copy((real_hbm, imag_hbm)[c].at[row], held.at[c, row], load_sem.at[c, row])
        for c, row in pieces
    ]
    stores = [
        pltpu.make_async_copy(held.at[c, row], out_hbm.at[c, row], store_sem.at[c, row])
        for c, row in pieces
    ]
    for load in loads:
        load.start()
    for load, store in zip(loads, stores):
        load.wait()
        store.start()
    for store in stores:
        store.wait()


def local(field, gain, spectral_phase):
    hbm_spec = pl.BlockSpec(memory_space=pltpu.HBM)
    real, imag = pl.pallas_call(
        kernel,
        out_shape=[jax.ShapeDtypeStruct((ROWS, COLS, N), BF16)] * 2,
        in_specs=[
            hbm_spec,
            hbm_spec,
            hbm_spec,
            hbm_spec,
            hbm_spec,
        ],
        out_specs=[hbm_spec] * 2,
        scratch_shapes=[
            pltpu.VMEM((2, ROWS, COLS, N), BF16),
            pltpu.VMEM((2, ROWS * COLS, N), BF16),
            pltpu.VMEM((2, N, N), BF16),
            pltpu.VMEM((2, 8, 128), F32),
            pltpu.VMEM((2, 2, N, N), BF16),
            pltpu.VMEM((ROWS, COLS), F32),
            pltpu.SMEM((N,), F32),
            pltpu.VMEM((COLS, ROWS), F32),
            pltpu.VMEM((2 * ROWS * ROW_STRIDE, COLS), F32),
            pltpu.VMEM((2, DEV, 2 * ROWS, COLS), BF16),
            pltpu.VMEM((2, DEV, 2 * ROWS, COLS), BF16),
            pltpu.VMEM((2, N, N), BF16),
            pltpu.VMEM((2, DEV, 2 * ROWS, COLS), BF16),
            pltpu.VMEM((2, DEV, 2 * ROWS, COLS), BF16),
            pltpu.VMEM((ROWS * COLS, N), F32),
            pltpu.VMEM((ROWS * COLS, N), F32),
            pltpu.SemaphoreType.DMA((8,)),
            pltpu.SemaphoreType.DMA((4,)),
            pltpu.SemaphoreType.DMA((6,)),
            pltpu.SemaphoreType.DMA((ROWS // 2, 2)),
        ],
        compiler_params=pltpu.CompilerParams(
            collective_id=0, has_side_effects=True, vmem_limit_bytes=56 << 20
        ),
    )(
        field,
        gain,
        spectral_phase,
        jnp.asarray(time_tables()),
        jnp.asarray(line_kernels()),
    )
    return pl.pallas_call(
        gather_parts,
        out_shape=jax.ShapeDtypeStruct((2, ROWS, COLS, N), BF16),
        in_specs=[hbm_spec] * 2,
        out_specs=hbm_spec,
        scratch_shapes=[
            pltpu.VMEM((2, ROWS, COLS, N), BF16),
            pltpu.SemaphoreType.DMA((2, ROWS)),
            pltpu.SemaphoreType.DMA((2, ROWS)),
        ],
        compiler_params=pltpu.CompilerParams(vmem_limit_bytes=56 << 20),
    )(real, imag)


def solution(mesh):
    in_specs = (P(None, "wide", "narrow", None), P("wide", "narrow"), P())
    out_specs = P(None, "wide", "narrow", None)
    return jax.shard_map(local, mesh=mesh, in_specs=in_specs, out_specs=out_specs, check_vma=False)
```

```python
import math

import jax
import jax.numpy as jnp
import numpy as np
from jax import lax
from jax.experimental import pallas as pl
from jax.experimental.pallas import tpu as pltpu
from jax.sharding import PartitionSpec as P

MESH = pl.DeviceIdType.MESH
BF16 = jnp.bfloat16
F32 = jnp.float32

N = 512
DEV = 256
HALF = N // 2
WIDE = 64
NARROW = 4
ROWS = 8
COLS = 128
KERR = 0.25
SATURATION = 1.0
DIFFRACT = 120.0
SEND_UNROLL = 1
ROW_STRIDE = DEV + 8

def _fit(func, count):
    nodes = 0.125 * (1.0 - np.cos((np.arange(400) + 0.5) * np.pi / 400))
    powers = nodes[:, None] ** np.arange(count)[None, :]
    return [float(v) for v in np.linalg.lstsq(powers, func(np.sqrt(nodes)), rcond=None)[0]]


SIN_TERMS = _fit(lambda z: np.sin(2 * np.pi * z) / z, 6)
COS_TERMS = _fit(lambda z: np.cos(2 * np.pi * z), 6)


def horner(terms, value):
    total = terms[-1]
    for term in terms[-2::-1]:
        total = total * value + term
    return total


def dft_tables(count):
    index = np.arange(count)
    angle = (index[:, None] * index[None, :] % count) * (2.0 * math.pi / count)
    factor = 1.0 / math.sqrt(count)
    return np.cos(angle) * factor, np.sin(angle) * factor


def signed_freq(index, count):
    return np.where(index < count // 2, index, index - count) / count


def time_tables():
    cos_table, sin_table = dft_tables(N)
    tables = []
    for part in range(2):
        cos_part = cos_table[part::2, :HALF]
        sin_part = sin_table[part::2, :HALF]
        tables.append(np.block([[cos_part, sin_part], [-sin_part, cos_part]]))
    return np.stack(tables).astype(BF16)


def line_kernels():
    index = np.arange(N)
    wave = signed_freq(index, N)
    chirp = np.exp(-1j * DIFFRACT * (wave * wave)[None, :] / (1.0 + 0.5 * wave)[:, None])
    lines = np.fft.ifft(chirp, axis=1)
    return np.stack([lines.real, lines.imag], axis=1).reshape(N, 8, 128).astype(np.float32)


def kernel(
    field_hbm,
    gain_hbm,
    phase_hbm,
    table_hbm,
    lines_hbm,
    real_hbm,
    imag_hbm,
    field,
    kerr,
    table,
    lines,
    circ,
    gain_ref,
    phase_ref,
    gain_t,
    spread,
    send1,
    recv1,
    plane,
    send2,
    recv2,
    even,
    odd,
    load_sem,
    send_sem,
    recv_sem,
    store_sem,
):
    wide = lax.axis_index("wide")
    narrow = lax.axis_index("narrow")
    me = wide * NARROW + narrow
    place = narrow * WIDE + wide

    barrier = pltpu.get_barrier_semaphore()

    fields = []
    for pair in range(ROWS // 2):
        at = pl.ds(2 * pair, 2)
        fields.append(pltpu.make_async_copy(field_hbm.at[:, at], field.at[:, at], load_sem.at[pair]))
    loads = [
        pltpu.make_async_copy(table_hbm, table, load_sem.at[4]),
        pltpu.make_async_copy(lines_hbm.at[pl.ds(2 * place, 2)], lines, load_sem.at[5]),
        pltpu.make_async_copy(phase_hbm, phase_ref, load_sem.at[7]),
    ]
    load_gain = pltpu.make_async_copy(gain_hbm, gain_ref, load_sem.at[6])
    for load in [load_gain] + fields + loads:
        load.start()

    @pl.loop(1, DEV)
    def _(step):
        other = lax.rem(me + step, DEV)
        pl.semaphore_signal(
            barrier, inc=1, device_id=(other // NARROW, lax.rem(other, NARROW)), device_id_type=MESH
        )

    load_gain.wait()
    gain_t[...] = jnp.transpose(gain_ref[...])
    block = 32

    def kerr_pair(pair):
        @pl.loop(0, 2 * COLS // block, unroll=4)
        def _(step):
            row = 2 * pair + step // (COLS // block)
            col = pl.multiple_of(lax.rem(step, COLS // block) * block, block)
            real = field[0, row, pl.ds(col, block), :].astype(F32)
            imag = field[1, row, pl.ds(col, block), :].astype(F32)
            intensity = real * real + imag * imag
            fluence = jnp.sum(intensity, axis=1, keepdims=True) * (1.0 / N)
            gains = gain_t[pl.ds(col, block), :]
            lane = lax.broadcasted_iota(jnp.int32, gains.shape, 1)
            gain = jnp.sum(jnp.where(lane == row, gains, 0.0), axis=1, keepdims=True)
            amplitude = jnp.exp(gain / (1.0 + fluence / SATURATION))
            turns = intensity * (KERR / (2.0 * math.pi))
            turns = turns - jnp.round(turns)
            square = turns * turns
            sin_kerr = amplitude * turns * horner(SIN_TERMS, square)
            cos_kerr = amplitude * horner(COS_TERMS, square)
            kerr_real = real * cos_kerr - imag * sin_kerr
            kerr_imag = real * sin_kerr + imag * cos_kerr
            at = pl.ds(pl.multiple_of(pair * 2 * COLS + step * block, block), block)
            for c, value in enumerate((kerr_real, kerr_imag)):
                first = value[:, :HALF]
                second = value[:, HALF:]
                kerr[0, at, c * HALF : (c + 1) * HALF] = (first + second).astype(BF16)
                kerr[1, at, c * HALF : (c + 1) * HALF] = (first - second).astype(BF16)

    def pair_rows(pair):
        return pl.ds(pl.multiple_of(pair * 2 * COLS, 2 * COLS), 2 * COLS)

    def time_forward(part, pair):
        at = pair_rows(pair)
        spectrum = lax.dot_general(
            table[part], kerr[part, at, :], (((1,), (1,)), ((), ())), preferred_element_type=F32
        )
        for c in range(2):
            for r in range(2):
                start = pl.multiple_of((c * ROWS + pair * 2 + r) * ROW_STRIDE, 8)
                spread[pl.ds(start, DEV), :] = spectrum[
                    c * DEV : (c + 1) * DEV, r * COLS : (r + 1) * COLS
                ]

    def gather_tile(index):
        parts = [
            spread[pl.ds(c * ROWS * ROW_STRIDE + index, ROWS, stride=ROW_STRIDE), :] for c in range(2)
        ]
        return jnp.concatenate(parts, axis=0).astype(BF16)

    def partner(step):
        other_wide = lax.rem(wide + step, WIDE)
        turn = step // WIDE
        other_chip = lax.rem(narrow // 2 + turn // 2, 2)
        other_core = lax.rem(narrow + turn, 2)
        other_narrow = other_chip * 2 + other_core
        return other_wide, other_narrow, other_narrow * WIDE + other_wide

    def partner_low_first(step):
        turn = lax.rem(step, WIDE)
        other_y, turn = turn // 16, lax.rem(turn, 16)
        z_turn, turn = turn // 4, lax.rem(turn, 4)
        core_turn = turn // 2
        other_x = lax.rem(wide // 32 + turn, 2)
        other_z = lax.rem(wide // 4 + z_turn, 4) + step // WIDE * 4
        other_wide = other_x * 32 + other_z * 4 + other_y
        other_narrow = lax.rem(narrow // 2 + 1, 2) * 2 + lax.rem(narrow + core_turn, 2)
        return other_wide, other_narrow, other_narrow * WIDE + other_wide

    def send_spectrum(part):
        @pl.loop(1, DEV, unroll=SEND_UNROLL)
        def _(step):
            other_wide, other_narrow, other = partner(step)
            send1[part, other] = gather_tile(other)
            pltpu.make_async_remote_copy(
                src_ref=send1.at[part, other],
                dst_ref=recv1.at[part, place],
                send_sem=send_sem.at[part],
                recv_sem=recv_sem.at[part],
                device_id=(other_wide, other_narrow),
                device_id_type=MESH,
            ).start()

        recv1[part, place] = gather_tile(place)

    def make_circulant(part):
        half_phase = 0.5 * phase_ref[2 * place + part]
        angle = jnp.full((1, N), half_phase, F32)
        cos_half = jnp.cos(angle)
        sin_half = jnp.sin(angle)
        real = jnp.concatenate([lines[part, j : j + 1, :] for j in range(4)], axis=1)
        imag = jnp.concatenate([lines[part, 4 + j : 5 + j, :] for j in range(4)], axis=1)
        turned = (real * cos_half - imag * sin_half, real * sin_half + imag * cos_half)
        for c in range(2):
            first = pltpu.roll(
                jnp.broadcast_to(turned[c], (COLS, N)), 0, 1, stride=1, stride_axis=0
            ).astype(BF16)
            for j in range(4):
                for k in range(4):
                    source = (k - j) % 4
                    circ[part, c, j * COLS : (j + 1) * COLS, k * COLS : (k + 1) * COLS] = first[
                        :, source * COLS : (source + 1) * COLS
                    ]

    def transform_plane(part):
        real_circ = circ[part, 0]
        imag_circ = circ[part, 1]
        group = 16

        @pl.loop(0, WIDE // group)
        def _(step):
            at = pl.multiple_of(step * group, group)
            lines_in = jnp.concatenate(
                [
                    recv1[part, pl.ds(j * WIDE + at, group)].reshape(group * 2 * ROWS, COLS)
                    for j in range(NARROW)
                ],
                axis=1,
            )
            by_real = jnp.dot(lines_in, real_circ, preferred_element_type=F32)
            by_imag = jnp.dot(lines_in, imag_circ, preferred_element_type=F32)
            by_real = by_real.reshape(group, 2, ROWS, N)
            by_imag = by_imag.reshape(group, 2, ROWS, N)
            rows = pl.ds(pl.multiple_of(step * group * ROWS, group * ROWS), group * ROWS)
            real = by_real[:, 0] - by_imag[:, 1]
            imag = by_imag[:, 0] + by_real[:, 1]
            plane[0, rows, :] = real.reshape(group * ROWS, N).astype(BF16)
            plane[1, rows, :] = imag.reshape(group * ROWS, N).astype(BF16)

        for half in range(2):
            cols = slice(half * 2 * COLS, (half + 1) * 2 * COLS)
            real_in = plane[0, :, cols]
            imag_in = plane[1, :, cols]
            real = jnp.dot(real_circ, real_in, preferred_element_type=F32) - jnp.dot(
                imag_circ, imag_in, preferred_element_type=F32
            )
            imag = jnp.dot(imag_circ, real_in, preferred_element_type=F32) + jnp.dot(
                real_circ, imag_in, preferred_element_type=F32
            )
            both = jnp.concatenate(
                [real.reshape(WIDE, ROWS, 2 * COLS), imag.reshape(WIDE, ROWS, 2 * COLS)], axis=1
            ).astype(BF16)
            for j in range(2):
                at = (2 * half + j) * WIDE
                send2[part, at : at + WIDE] = both[:, :, j * COLS : (j + 1) * COLS]

    def send_back(part):
        for half in range(2):

            @pl.loop(max(1, half * DEV // 2), (half + 1) * DEV // 2, unroll=SEND_UNROLL)
            def _(step):
                if part == 1 and half == 1:
                    other_wide, other_narrow, other = partner_low_first(step - DEV // 2)
                else:
                    other_wide, other_narrow, other = partner(step)
                pltpu.make_async_remote_copy(
                    src_ref=send2.at[part, other],
                    dst_ref=recv2.at[part, place],
                    send_sem=send_sem.at[2 + part],
                    recv_sem=recv_sem.at[2 + 2 * part + half],
                    device_id=(other_wide, other_narrow),
                    device_id_type=MESH,
                ).start()

        recv2[part, place] = send2[part, place]

    def wait_bytes(buffer, part, sem, count=DEV - 1):
        view = buffer.at[part, pl.ds(0, count)]
        pltpu.make_async_copy(view, view, sem).wait()

    def stores(pair):
        at = pl.ds(pair * 2, 2)
        return [
            pltpu.make_async_copy(field.at[c, at], out.at[at], store_sem.at[pair, c])
            for c, out in enumerate((real_hbm, imag_hbm))
        ]

    def unpack(part, start, count):
        @pl.loop(0, count, unroll=8)
        def _(step):
            index = start + step
            tile = recv2[part, index].astype(F32)
            for c in range(2):
                spread[pl.ds(c * ROWS * ROW_STRIDE + index, ROWS, stride=ROW_STRIDE), :] = tile[
                    c * ROWS : (c + 1) * ROWS
                ]

    def time_inverse(part, pair, start, count):
        columns = []
        for r in range(2):
            pieces = []
            for c in range(2):
                base = pl.multiple_of((c * ROWS + pair * 2 + r) * ROW_STRIDE + start, 8)
                pieces.append(spread[pl.ds(base, count), :])
            columns.append(jnp.concatenate(pieces, axis=0))
        spectrum = jnp.concatenate(columns, axis=1).astype(BF16)
        rows = [table[part, pl.ds(pl.multiple_of(c * DEV + start, WIDE), count), :] for c in range(2)]
        return lax.dot_general(
            spectrum,
            jnp.concatenate(rows, axis=0),
            (((0,), (0,)), ((), ())),
            preferred_element_type=F32,
        )

    def inverse_even():
        unpack(0, 0, DEV)

        @pl.loop(0, ROWS // 2)
        def _(pair):
            even[pair_rows(pair), :] = time_inverse(0, pair, 0, DEV)

    def inverse_odd(half):
        start = pl.multiple_of(lax.rem(narrow // 2 + half, 2) * 2 * WIDE, 2 * WIDE)
        unpack(1, start, 2 * WIDE)

        @pl.loop(0, ROWS // 2)
        def _(pair):
            at = pair_rows(pair)
            result = time_inverse(1, pair, start, 2 * WIDE)
            if half == 0:
                odd[at, :] = result
                return
            result = result + odd[at, :]
            first = even[at, :]
            for j, value in enumerate((first + result, first - result)):
                value = value.astype(BF16)
                for r in range(2):
                    for c in range(2):
                        field[c, pair * 2 + r, :, j * HALF : (j + 1) * HALF] = value[
                            r * COLS : (r + 1) * COLS, c * HALF : (c + 1) * HALF
                        ]
            for store in stores(pair):
                store.start()

    for pair in range(ROWS // 2):
        fields[pair].wait()
        kerr_pair(pair)
        if pair == 0:
            loads[0].wait()
        time_forward(0, pair)

    pl.semaphore_wait(barrier, DEV - 1)
    send_spectrum(0)

    @pl.loop(0, ROWS // 2)
    def _(pair):
        time_forward(1, pair)

    send_spectrum(1)
    loads[1].wait()
    loads[2].wait()
    for part in range(2):
        make_circulant(part)
    for part in range(2):
        wait_bytes(recv1, part, recv_sem.at[part])
        transform_plane(part)
        send_back(part)
    wait_bytes(recv2, 0, recv_sem.at[2], DEV // 2 - 1)
    wait_bytes(recv2, 0, recv_sem.at[3], DEV // 2)
    inverse_even()
    wait_bytes(recv2, 1, recv_sem.at[4], DEV // 2 - 1)
    inverse_odd(0)
    wait_bytes(recv2, 1, recv_sem.at[5], DEV // 2)
    inverse_odd(1)
    for pair in range(ROWS // 2):
        for store in stores(pair):
            store.wait()
    for part in range(2):
        wait_bytes(send1, part, send_sem.at[part])
        wait_bytes(send2, part, send_sem.at[2 + part])


def gather_parts(real_hbm, imag_hbm, out_hbm, held, load_sem, store_sem):
    pieces = [(c, pl.ds(row, 4)) for row in range(0, ROWS, 4) for c in range(2)]
    loads = [
        pltpu.make_async_copy((real_hbm, imag_hbm)[c].at[row], held.at[c, row], load_sem.at[k])
        for k, (c, row) in enumerate(pieces)
    ]
    stores = [
        pltpu.make_async_copy(held.at[c, row], out_hbm.at[c, row], store_sem.at[k])
        for k, (c, row) in enumerate(pieces)
    ]
    for load in loads:
        load.start()
    for load, store in zip(loads, stores):
        load.wait()
        store.start()
    for store in stores:
        store.wait()


def local(field, gain, spectral_phase):
    hbm_spec = pl.BlockSpec(memory_space=pltpu.HBM)
    real, imag = pl.pallas_call(
        kernel,
        out_shape=[jax.ShapeDtypeStruct((ROWS, COLS, N), BF16)] * 2,
        in_specs=[
            hbm_spec,
            hbm_spec,
            hbm_spec,
            hbm_spec,
            hbm_spec,
        ],
        out_specs=[hbm_spec] * 2,
        scratch_shapes=[
            pltpu.VMEM((2, ROWS, COLS, N), BF16),
            pltpu.VMEM((2, ROWS * COLS, N), BF16),
            pltpu.VMEM((2, N, N), BF16),
            pltpu.VMEM((2, 8, 128), F32),
            pltpu.VMEM((2, 2, N, N), BF16),
            pltpu.VMEM((ROWS, COLS), F32),
            pltpu.SMEM((N,), F32),
            pltpu.VMEM((COLS, ROWS), F32),
            pltpu.VMEM((2 * ROWS * ROW_STRIDE, COLS), F32),
            pltpu.VMEM((2, DEV, 2 * ROWS, COLS), BF16),
            pltpu.VMEM((2, DEV, 2 * ROWS, COLS), BF16),
            pltpu.VMEM((2, N, N), BF16),
            pltpu.VMEM((2, DEV, 2 * ROWS, COLS), BF16),
            pltpu.VMEM((2, DEV, 2 * ROWS, COLS), BF16),
            pltpu.VMEM((ROWS * COLS, N), F32),
            pltpu.VMEM((ROWS * COLS, N), F32),
            pltpu.SemaphoreType.DMA((8,)),
            pltpu.SemaphoreType.DMA((4,)),
            pltpu.SemaphoreType.DMA((6,)),
            pltpu.SemaphoreType.DMA((ROWS // 2, 2)),
        ],
        compiler_params=pltpu.CompilerParams(
            collective_id=0, has_side_effects=True, vmem_limit_bytes=56 << 20
        ),
    )(
        field,
        gain,
        spectral_phase,
        jnp.asarray(time_tables()),
        jnp.asarray(line_kernels()),
    )
    return pl.pallas_call(
        gather_parts,
        out_shape=jax.ShapeDtypeStruct((2, ROWS, COLS, N), BF16),
        in_specs=[hbm_spec] * 2,
        out_specs=hbm_spec,
        scratch_shapes=[
            pltpu.VMEM((2, ROWS, COLS, N), BF16),
            pltpu.SemaphoreType.DMA((2 * ROWS,)),
            pltpu.SemaphoreType.DMA((2 * ROWS,)),
        ],
        compiler_params=pltpu.CompilerParams(vmem_limit_bytes=56 << 20),
    )(real, imag)


def solution(mesh):
    in_specs = (P(None, "wide", "narrow", None), P("wide", "narrow"), P())
    out_specs = P(None, "wide", "narrow", None)
    return jax.shard_map(local, mesh=mesh, in_specs=in_specs, out_specs=out_specs, check_vma=False)
```

```python
import math

import jax
import jax.numpy as jnp
import numpy as np
from jax import lax
from jax.experimental import pallas as pl
from jax.experimental.pallas import tpu as pltpu
from jax.sharding import PartitionSpec as P

MESH = pl.DeviceIdType.MESH
BF16 = jnp.bfloat16
F32 = jnp.float32

N = 512
DEV = 256
HALF = N // 2
WIDE = 64
NARROW = 4
ROWS = 8
COLS = 128
KERR = 0.25
SATURATION = 1.0
DIFFRACT = 120.0
SEND_UNROLL = 1
ROW_STRIDE = DEV + 8

def _fit(func, count):
    nodes = 0.125 * (1.0 - np.cos((np.arange(400) + 0.5) * np.pi / 400))
    powers = nodes[:, None] ** np.arange(count)[None, :]
    return [float(v) for v in np.linalg.lstsq(powers, func(np.sqrt(nodes)), rcond=None)[0]]


SIN_TERMS = _fit(lambda z: np.sin(2 * np.pi * z) / z, 6)
COS_TERMS = _fit(lambda z: np.cos(2 * np.pi * z), 6)


def horner(terms, value):
    total = terms[-1]
    for term in terms[-2::-1]:
        total = total * value + term
    return total


def dft_tables(count):
    index = np.arange(count)
    angle = (index[:, None] * index[None, :] % count) * (2.0 * math.pi / count)
    factor = 1.0 / math.sqrt(count)
    return np.cos(angle) * factor, np.sin(angle) * factor


def signed_freq(index, count):
    return np.where(index < count // 2, index, index - count) / count


def time_tables():
    cos_table, sin_table = dft_tables(N)
    tables = []
    for part in range(2):
        cos_part = cos_table[part::2, :HALF]
        sin_part = sin_table[part::2, :HALF]
        tables.append(np.block([[cos_part, sin_part], [-sin_part, cos_part]]))
    return np.stack(tables).astype(BF16)


def line_kernels():
    index = np.arange(N)
    wave = signed_freq(index, N)
    chirp = np.exp(-1j * DIFFRACT * (wave * wave)[None, :] / (1.0 + 0.5 * wave)[:, None])
    lines = np.fft.ifft(chirp, axis=1)
    return np.stack([lines.real, lines.imag], axis=1).reshape(N, 8, 128).astype(np.float32)


def kernel(
    field_hbm,
    gain_hbm,
    phase_hbm,
    table_hbm,
    lines_hbm,
    real_hbm,
    imag_hbm,
    field,
    kerr,
    table,
    lines,
    circ,
    gain_ref,
    phase_ref,
    gain_t,
    spread,
    send1,
    recv1,
    plane,
    send2,
    recv2,
    even,
    odd,
    load_sem,
    send_sem,
    recv_sem,
    store_sem,
):
    wide = lax.axis_index("wide")
    narrow = lax.axis_index("narrow")
    me = wide * NARROW + narrow
    place = narrow * WIDE + wide

    barrier = pltpu.get_barrier_semaphore()

    fields = []
    for pair in range(ROWS // 2):
        at = pl.ds(2 * pair, 2)
        fields.append(pltpu.make_async_copy(field_hbm.at[:, at], field.at[:, at], load_sem.at[pair]))
    loads = [
        pltpu.make_async_copy(table_hbm, table, load_sem.at[4]),
        pltpu.make_async_copy(lines_hbm.at[pl.ds(2 * place, 2)], lines, load_sem.at[5]),
        pltpu.make_async_copy(phase_hbm, phase_ref, load_sem.at[7]),
    ]
    load_gain = pltpu.make_async_copy(gain_hbm, gain_ref, load_sem.at[6])
    for load in [load_gain] + fields + loads:
        load.start()

    @pl.loop(1, DEV)
    def _(step):
        other = lax.rem(me + step, DEV)
        pl.semaphore_signal(
            barrier, inc=1, device_id=(other // NARROW, lax.rem(other, NARROW)), device_id_type=MESH
        )

    load_gain.wait()
    gain_t[...] = jnp.transpose(gain_ref[...])
    block = 32

    def kerr_pair(pair):
        @pl.loop(0, 2 * COLS // block, unroll=4)
        def _(step):
            row = 2 * pair + step // (COLS // block)
            col = pl.multiple_of(lax.rem(step, COLS // block) * block, block)
            real = field[0, row, pl.ds(col, block), :].astype(F32)
            imag = field[1, row, pl.ds(col, block), :].astype(F32)
            intensity = real * real + imag * imag
            fluence = jnp.sum(intensity, axis=1, keepdims=True) * (1.0 / N)
            gains = gain_t[pl.ds(col, block), :]
            lane = lax.broadcasted_iota(jnp.int32, gains.shape, 1)
            gain = jnp.sum(jnp.where(lane == row, gains, 0.0), axis=1, keepdims=True)
            amplitude = jnp.exp(gain / (1.0 + fluence / SATURATION))
            turns = intensity * (KERR / (2.0 * math.pi))
            turns = turns - jnp.round(turns)
            square = turns * turns
            sin_kerr = amplitude * turns * horner(SIN_TERMS, square)
            cos_kerr = amplitude * horner(COS_TERMS, square)
            kerr_real = real * cos_kerr - imag * sin_kerr
            kerr_imag = real * sin_kerr + imag * cos_kerr
            at = pl.ds(pl.multiple_of(pair * 2 * COLS + step * block, block), block)
            for c, value in enumerate((kerr_real, kerr_imag)):
                first = value[:, :HALF]
                second = value[:, HALF:]
                kerr[0, at, c * HALF : (c + 1) * HALF] = (first + second).astype(BF16)
                kerr[1, at, c * HALF : (c + 1) * HALF] = (first - second).astype(BF16)

    def pair_rows(pair):
        return pl.ds(pl.multiple_of(pair * 2 * COLS, 2 * COLS), 2 * COLS)

    def time_forward(part, pair):
        at = pair_rows(pair)
        spectrum = lax.dot_general(
            table[part], kerr[part, at, :], (((1,), (1,)), ((), ())), preferred_element_type=F32
        )
        for c in range(2):
            for r in range(2):
                start = pl.multiple_of((c * ROWS + pair * 2 + r) * ROW_STRIDE, 8)
                spread[pl.ds(start, DEV), :] = spectrum[
                    c * DEV : (c + 1) * DEV, r * COLS : (r + 1) * COLS
                ]

    def gather_tile(index):
        parts = [
            spread[pl.ds(c * ROWS * ROW_STRIDE + index, ROWS, stride=ROW_STRIDE), :] for c in range(2)
        ]
        return jnp.concatenate(parts, axis=0).astype(BF16)

    def partner(step):
        other_wide = lax.rem(wide + step, WIDE)
        turn = step // WIDE
        other_chip = lax.rem(narrow // 2 + turn // 2, 2)
        other_core = lax.rem(narrow + turn, 2)
        other_narrow = other_chip * 2 + other_core
        return other_wide, other_narrow, other_narrow * WIDE + other_wide

    def partner_low_first(step):
        turn = lax.rem(step, WIDE)
        other_y, turn = turn // 16, lax.rem(turn, 16)
        z_turn, turn = turn // 4, lax.rem(turn, 4)
        core_turn = turn // 2
        other_x = lax.rem(wide // 32 + turn, 2)
        other_z = lax.rem(wide // 4 + z_turn, 4) + step // WIDE * 4
        other_wide = other_x * 32 + other_z * 4 + other_y
        other_narrow = lax.rem(narrow // 2 + 1, 2) * 2 + 1 - core_turn
        return other_wide, other_narrow, other_narrow * WIDE + other_wide

    def send_spectrum(part):
        @pl.loop(1, DEV, unroll=SEND_UNROLL)
        def _(step):
            other_wide, other_narrow, other = partner(step)
            send1[part, other] = gather_tile(other)
            pltpu.make_async_remote_copy(
                src_ref=send1.at[part, other],
                dst_ref=recv1.at[part, place],
                send_sem=send_sem.at[part],
                recv_sem=recv_sem.at[part],
                device_id=(other_wide, other_narrow),
                device_id_type=MESH,
            ).start()

        recv1[part, place] = gather_tile(place)

    def make_circulant(part):
        half_phase = 0.5 * phase_ref[2 * place + part]
        angle = jnp.full((1, N), half_phase, F32)
        cos_half = jnp.cos(angle)
        sin_half = jnp.sin(angle)
        real = jnp.concatenate([lines[part, j : j + 1, :] for j in range(4)], axis=1)
        imag = jnp.concatenate([lines[part, 4 + j : 5 + j, :] for j in range(4)], axis=1)
        turned = (real * cos_half - imag * sin_half, real * sin_half + imag * cos_half)
        for c in range(2):
            first = pltpu.roll(
                jnp.broadcast_to(turned[c], (COLS, N)), 0, 1, stride=1, stride_axis=0
            ).astype(BF16)
            for j in range(4):
                for k in range(4):
                    source = (k - j) % 4
                    circ[part, c, j * COLS : (j + 1) * COLS, k * COLS : (k + 1) * COLS] = first[
                        :, source * COLS : (source + 1) * COLS
                    ]

    def transform_plane(part):
        real_circ = circ[part, 0]
        imag_circ = circ[part, 1]
        group = 16

        @pl.loop(0, WIDE // group)
        def _(step):
            at = pl.multiple_of(step * group, group)
            lines_in = jnp.concatenate(
                [
                    recv1[part, pl.ds(j * WIDE + at, group)].reshape(group * 2 * ROWS, COLS)
                    for j in range(NARROW)
                ],
                axis=1,
            )
            by_real = jnp.dot(lines_in, real_circ, preferred_element_type=F32)
            by_imag = jnp.dot(lines_in, imag_circ, preferred_element_type=F32)
            by_real = by_real.reshape(group, 2, ROWS, N)
            by_imag = by_imag.reshape(group, 2, ROWS, N)
            rows = pl.ds(pl.multiple_of(step * group * ROWS, group * ROWS), group * ROWS)
            real = by_real[:, 0] - by_imag[:, 1]
            imag = by_imag[:, 0] + by_real[:, 1]
            plane[0, rows, :] = real.reshape(group * ROWS, N).astype(BF16)
            plane[1, rows, :] = imag.reshape(group * ROWS, N).astype(BF16)

        for half in range(2):
            cols = slice(half * 2 * COLS, (half + 1) * 2 * COLS)
            real_in = plane[0, :, cols]
            imag_in = plane[1, :, cols]
            real = jnp.dot(real_circ, real_in, preferred_element_type=F32) - jnp.dot(
                imag_circ, imag_in, preferred_element_type=F32
            )
            imag = jnp.dot(imag_circ, real_in, preferred_element_type=F32) + jnp.dot(
                real_circ, imag_in, preferred_element_type=F32
            )
            both = jnp.concatenate(
                [real.reshape(WIDE, ROWS, 2 * COLS), imag.reshape(WIDE, ROWS, 2 * COLS)], axis=1
            ).astype(BF16)
            for j in range(2):
                at = (2 * half + j) * WIDE
                send2[part, at : at + WIDE] = both[:, :, j * COLS : (j + 1) * COLS]

    def send_back(part):
        for half in range(2):

            @pl.loop(max(1, half * DEV // 2), (half + 1) * DEV // 2, unroll=SEND_UNROLL)
            def _(step):
                if part == 1 and half == 1:
                    other_wide, other_narrow, other = partner_low_first(step - DEV // 2)
                else:
                    other_wide, other_narrow, other = partner(step)
                pltpu.make_async_remote_copy(
                    src_ref=send2.at[part, other],
                    dst_ref=recv2.at[part, place],
                    send_sem=send_sem.at[2 + part],
                    recv_sem=recv_sem.at[2 + 2 * part + half],
                    device_id=(other_wide, other_narrow),
                    device_id_type=MESH,
                ).start()

        recv2[part, place] = send2[part, place]

    def wait_bytes(buffer, part, sem, count=DEV - 1):
        view = buffer.at[part, pl.ds(0, count)]
        pltpu.make_async_copy(view, view, sem).wait()

    def stores(pair):
        at = pl.ds(pair * 2, 2)
        return [
            pltpu.make_async_copy(field.at[c, at], out.at[at], store_sem.at[pair, c])
            for c, out in enumerate((real_hbm, imag_hbm))
        ]

    def unpack(part, start, count):
        @pl.loop(0, count, unroll=8)
        def _(step):
            index = start + step
            tile = recv2[part, index].astype(F32)
            for c in range(2):
                spread[pl.ds(c * ROWS * ROW_STRIDE + index, ROWS, stride=ROW_STRIDE), :] = tile[
                    c * ROWS : (c + 1) * ROWS
                ]

    def time_inverse(part, pair, start, count):
        columns = []
        for r in range(2):
            pieces = []
            for c in range(2):
                base = pl.multiple_of((c * ROWS + pair * 2 + r) * ROW_STRIDE + start, 8)
                pieces.append(spread[pl.ds(base, count), :])
            columns.append(jnp.concatenate(pieces, axis=0))
        spectrum = jnp.concatenate(columns, axis=1).astype(BF16)
        rows = [table[part, pl.ds(pl.multiple_of(c * DEV + start, WIDE), count), :] for c in range(2)]
        return lax.dot_general(
            spectrum,
            jnp.concatenate(rows, axis=0),
            (((0,), (0,)), ((), ())),
            preferred_element_type=F32,
        )

    def inverse_even():
        unpack(0, 0, DEV)

        @pl.loop(0, ROWS // 2)
        def _(pair):
            even[pair_rows(pair), :] = time_inverse(0, pair, 0, DEV)

    def inverse_odd(half):
        start = pl.multiple_of(lax.rem(narrow // 2 + half, 2) * 2 * WIDE, 2 * WIDE)
        unpack(1, start, 2 * WIDE)

        @pl.loop(0, ROWS // 2)
        def _(pair):
            at = pair_rows(pair)
            result = time_inverse(1, pair, start, 2 * WIDE)
            if half == 0:
                odd[at, :] = result
                return
            result = result + odd[at, :]
            first = even[at, :]
            for j, value in enumerate((first + result, first - result)):
                value = value.astype(BF16)
                for r in range(2):
                    for c in range(2):
                        field[c, pair * 2 + r, :, j * HALF : (j + 1) * HALF] = value[
                            r * COLS : (r + 1) * COLS, c * HALF : (c + 1) * HALF
                        ]
            for store in stores(pair):
                store.start()

    for pair in range(ROWS // 2):
        fields[pair].wait()
        kerr_pair(pair)
        if pair == 0:
            loads[0].wait()
        time_forward(0, pair)

    pl.semaphore_wait(barrier, DEV - 1)
    send_spectrum(0)

    @pl.loop(0, ROWS // 2)
    def _(pair):
        time_forward(1, pair)

    send_spectrum(1)
    loads[1].wait()
    loads[2].wait()
    for part in range(2):
        make_circulant(part)
    for part in range(2):
        wait_bytes(recv1, part, recv_sem.at[part])
        transform_plane(part)
        send_back(part)
    wait_bytes(recv2, 0, recv_sem.at[2], DEV // 2 - 1)
    wait_bytes(recv2, 0, recv_sem.at[3], DEV // 2)
    inverse_even()
    wait_bytes(recv2, 1, recv_sem.at[4], DEV // 2 - 1)
    inverse_odd(0)
    wait_bytes(recv2, 1, recv_sem.at[5], DEV // 2)
    inverse_odd(1)
    for pair in range(ROWS // 2):
        for store in stores(pair):
            store.wait()
    for part in range(2):
        wait_bytes(send1, part, send_sem.at[part])
        wait_bytes(send2, part, send_sem.at[2 + part])


def gather_parts(real_hbm, imag_hbm, out_hbm, held, load_sem, store_sem):
    pieces = [(c, pl.ds(row, 4)) for row in range(0, ROWS, 4) for c in range(2)]
    loads = [
        pltpu.make_async_copy((real_hbm, imag_hbm)[c].at[row], held.at[c, row], load_sem.at[k])
        for k, (c, row) in enumerate(pieces)
    ]
    stores = [
        pltpu.make_async_copy(held.at[c, row], out_hbm.at[c, row], store_sem.at[k])
        for k, (c, row) in enumerate(pieces)
    ]
    for load in loads:
        load.start()
    for load, store in zip(loads, stores):
        load.wait()
        store.start()
    for store in stores:
        store.wait()


def local(field, gain, spectral_phase):
    hbm_spec = pl.BlockSpec(memory_space=pltpu.HBM)
    real, imag = pl.pallas_call(
        kernel,
        out_shape=[jax.ShapeDtypeStruct((ROWS, COLS, N), BF16)] * 2,
        in_specs=[
            hbm_spec,
            hbm_spec,
            hbm_spec,
            hbm_spec,
            hbm_spec,
        ],
        out_specs=[hbm_spec] * 2,
        scratch_shapes=[
            pltpu.VMEM((2, ROWS, COLS, N), BF16),
            pltpu.VMEM((2, ROWS * COLS, N), BF16),
            pltpu.VMEM((2, N, N), BF16),
            pltpu.VMEM((2, 8, 128), F32),
            pltpu.VMEM((2, 2, N, N), BF16),
            pltpu.VMEM((ROWS, COLS), F32),
            pltpu.SMEM((N,), F32),
            pltpu.VMEM((COLS, ROWS), F32),
            pltpu.VMEM((2 * ROWS * ROW_STRIDE, COLS), F32),
            pltpu.VMEM((2, DEV, 2 * ROWS, COLS), BF16),
            pltpu.VMEM((2, DEV, 2 * ROWS, COLS), BF16),
            pltpu.VMEM((2, N, N), BF16),
            pltpu.VMEM((2, DEV, 2 * ROWS, COLS), BF16),
            pltpu.VMEM((2, DEV, 2 * ROWS, COLS), BF16),
            pltpu.VMEM((ROWS * COLS, N), F32),
            pltpu.VMEM((ROWS * COLS, N), F32),
            pltpu.SemaphoreType.DMA((8,)),
            pltpu.SemaphoreType.DMA((4,)),
            pltpu.SemaphoreType.DMA((6,)),
            pltpu.SemaphoreType.DMA((ROWS // 2, 2)),
        ],
        compiler_params=pltpu.CompilerParams(
            collective_id=0, has_side_effects=True, vmem_limit_bytes=56 << 20
        ),
    )(
        field,
        gain,
        spectral_phase,
        jnp.asarray(time_tables()),
        jnp.asarray(line_kernels()),
    )
    return pl.pallas_call(
        gather_parts,
        out_shape=jax.ShapeDtypeStruct((2, ROWS, COLS, N), BF16),
        in_specs=[hbm_spec] * 2,
        out_specs=hbm_spec,
        scratch_shapes=[
            pltpu.VMEM((2, ROWS, COLS, N), BF16),
            pltpu.SemaphoreType.DMA((2 * ROWS,)),
            pltpu.SemaphoreType.DMA((2 * ROWS,)),
        ],
        compiler_params=pltpu.CompilerParams(vmem_limit_bytes=56 << 20),
    )(real, imag)


def solution(mesh):
    in_specs = (P(None, "wide", "narrow", None), P("wide", "narrow"), P())
    out_specs = P(None, "wide", "narrow", None)
    return jax.shard_map(local, mesh=mesh, in_specs=in_specs, out_specs=out_specs, check_vma=False)
```
